32 devices in a mesh: section: 4 (over z), dp: 2 (over x), seq: 4 (over y, core).
Axes of the slice: x: 2, y: 2, z: 4, core: 2. Of those that a mesh axis runs over, the one named last changes fastest.
Arguments:
- incoming: bfloat16 [4, 2, 512, 4096], P('section', 'dp', 'seq'), may hold values from -6 to 6
- chosen: int32 [4, 2, 64], P('section', 'dp'), may hold values from 0 to 511, as said below
- norm_gain: float32 [4, 4096], P('section'), may hold values from 0.1 to 1.9
- router: bfloat16 [4, 4096], P('section'), may hold values from -0.25 to 0.25
- w_query: bfloat16 [4, 4096, 4096], P('section', 'dp', 'seq'), may hold values from -1 to 1
- w_key: bfloat16 [4, 4096, 4096], P('section', 'dp', 'seq'), may hold values from -1 to 1
- w_value: bfloat16 [4, 4096, 4096], P('section', 'dp', 'seq'), may hold values from -0.09375 to 0.09375
- w_out_t: bfloat16 [4, 4096, 4096], P('section', 'dp', 'seq'), may hold values from -0.5 to 0.5
Outputs:
- outgoing: bfloat16 [4, 2, 512, 4096], P('section', 'dp', 'seq')
The draws below stay inside these ranges and needn't reach their ends.
Inputs may be any that keep to these rules, and one draw needn't show every extreme that they name: chosen[s, b] holds 64 distinct positions in increasing order; each aligned block of 128 positions holds at most 32 of them, and in every sequence one block holds exactly 32.
All inputs are finite; a program needn't handle non-finite values.
Results may differ from the reference program's by a relative error of at most 0.014.
Values may be sent and summed in bfloat16 or wider, within the bound.
A program may use at most 128 MiB of HBM per device.

```python
import jax
import jax.numpy as jnp
from jax import lax

D = 4096
HEADS = 32
HD = 128
TOK_DEV = 128
SECTIONS = 4
BATCH = 2
LEN = 512
CHOSEN = 64
MOST = 32
N_SEQ = 4


def draw_chosen(key, part):
    shard_count = LEN // TOK_DEV
    row_count = SECTIONS * BATCH
    base_key = jax.random.fold_in(key, 11)
    key_heavy, key_weight, key_score = jax.random.split(base_key, 3)
    heavy_shard = jax.random.randint(key_heavy, (row_count, 1), 0, shard_count)
    shard_ids = jnp.arange(shard_count, dtype=jnp.int32)[None, :]
    is_heavy = shard_ids == heavy_shard
    shares = jax.random.randint(key_weight, (row_count, shard_count), 1, 3)
    shares = jnp.where(is_heavy, 0, shares)
    spare_rows = CHOSEN - MOST
    share_sum = jnp.sum(shares, axis=1, keepdims=True)
    floors = spare_rows * shares // share_sum
    leftover = spare_rows - jnp.sum(floors, axis=1, keepdims=True)
    others = 1 - is_heavy.astype(jnp.int32)
    slot_rank = jnp.cumsum(others, axis=1) - others
    extra_one = jnp.where((others == 1) & (slot_rank < leftover), 1, 0)
    counts = floors + extra_one + jnp.where(is_heavy, MOST, 0)
    scores = jax.random.randint(key_score, (row_count, shard_count, TOK_DEV), 0, 1 << 20) * TOK_DEV + jnp.arange(TOK_DEV, dtype=jnp.int32)
    order_ids = jnp.argsort(scores, axis=-1)
    rank_ids = jnp.argsort(order_ids, axis=-1)
    taken_mask = rank_ids < counts[:, :, None]
    flat_mask = taken_mask.reshape(row_count, LEN)
    sort_key = jnp.where(flat_mask, 0, LEN) + jnp.arange(LEN, dtype=jnp.int32)
    picked = jnp.argsort(sort_key, axis=-1)[:, :CHOSEN]
    return picked.astype(jnp.int32).reshape(SECTIONS, BATCH, CHOSEN)


def draw_w_query(key, part):
    drawn = jax.random.normal(jax.random.fold_in(key, 1), (SECTIONS, D, HEADS * HD), jnp.float32) * D ** (-0.5)
    return jnp.clip(drawn, -1.0, 1.0).astype(jnp.bfloat16)


def draw_w_key(key, part):
    drawn = jax.random.normal(jax.random.fold_in(key, 3), (SECTIONS, D, HEADS * HD), jnp.float32) * D ** (-0.5)
    return jnp.clip(drawn, -1.0, 1.0).astype(jnp.bfloat16)


def block_levels(stream_key, extent, cuts, low, largest):
    level = 1.0
    for dim, shards_of in cuts:
        draws = jax.random.uniform(jax.random.fold_in(jax.random.fold_in(stream_key, 6), dim), (shards_of,), jnp.float32, low / len(cuts), largest / len(cuts))
        level = level * jnp.repeat(jnp.exp(draws), extent[dim] // shards_of).reshape((-1,) + (1,) * (len(extent) - 1 - dim))
    return level


def centred(key, extent, deviation, most, cuts=(), held_as=jnp.bfloat16):
    result = deviation * jax.random.normal(key, extent, jnp.float32)
    if cuts:
        result = result * block_levels(key, extent, cuts, -0.22, 0.18)
    return jnp.clip(result, -most, most).astype(held_as)


def setup_inputs(seed: int = 0) -> dict:
    splits = jax.random.split(jax.random.key(seed), 9)
    incoming = centred(splits[0], (SECTIONS, BATCH, LEN, D), 1.0, 6.0, ((0, 4), (1, 2), (2, 4)))
    chosen = draw_chosen(jax.random.fold_in(splits[8], 71), 0)
    norm_gain = jnp.clip(1.0 + 0.18 * jax.random.normal(splits[2], (SECTIONS, D), jnp.float32), 0.1, 1.9)
    router = centred(splits[3], (SECTIONS, D), (D // 9) ** -0.5, 0.25, ((0, 4),))
    w_query = draw_w_query(jax.random.fold_in(splits[8], 71), 0)
    w_key = draw_w_key(jax.random.fold_in(splits[8], 71), 0)
    w_value = centred(splits[6], (SECTIONS, D, HEADS * HD), D ** -0.5, 0.09375, ((0, 4), (1, 2), (2, 4)))
    w_out_t = centred(splits[7], (SECTIONS, D, HEADS * HD), HD ** -0.5, 0.5, ((0, 4), (1, 2), (2, 4)))
    return {"incoming": incoming, "chosen": chosen, "norm_gain": norm_gain, "router": router, "w_query": w_query, "w_key": w_key, "w_value": w_value, "w_out_t": w_out_t}


EPSILON = 1e-05
ROPE_BASE = 500000.0
NEG_FILL = -1e+30

def rms_norm(rows_in, gain_vec):
    widened = rows_in.astype(jnp.float32)
    inv_scale = lax.rsqrt(lax.optimization_barrier(jnp.mean(widened * widened, axis=-1, keepdims=True)) + EPSILON)
    return (widened * inv_scale * gain_vec[None, :]).astype(jnp.bfloat16)

def apply_rope(projected, positions):
    half_dim = HD // 2
    inverse_freq = ROPE_BASE ** (-2.0 * jnp.arange(half_dim, dtype=jnp.float32) / HD)
    angles = positions.astype(jnp.float32)[:, None] * inverse_freq[None, :]
    cosine = jnp.cos(angles)[:, None, :]
    sine_vals = jnp.sin(angles)[:, None, :]
    shaped = projected.reshape(projected.shape[0], -1, HD)
    first_half = shaped[:, :, :half_dim]
    second_half = shaped[:, :, half_dim:]
    rotated = jnp.concatenate([first_half * cosine - second_half * sine_vals, second_half * cosine + first_half * sine_vals], axis=-1)
    return rotated.reshape(projected.shape)

def attend(queries, keys_in, values_in, query_pos, key_pos):
    heads_split = queries.reshape(queries.shape[0], -1, HD).astype(jnp.float32)
    keys_split = keys_in.reshape(keys_in.shape[0], -1, HD).astype(jnp.float32)
    values_split = values_in.reshape(values_in.shape[0], -1, HD).astype(jnp.float32)
    scores = jnp.einsum('qhd,khd->hqk', heads_split, keys_split) * HD ** (-0.5)
    allowed = key_pos[None, :] <= query_pos[:, None]
    scores = jnp.where(allowed[None, :, :], scores, NEG_FILL)
    peak_val = lax.optimization_barrier(jnp.max(scores, axis=-1, keepdims=True))
    exponent = jnp.exp(scores - peak_val)
    attn_weights = (exponent / lax.optimization_barrier(jnp.sum(exponent, axis=-1, keepdims=True))).astype(jnp.bfloat16)
    mixed = jnp.einsum('hqk,khd->qhd', attn_weights.astype(jnp.float32), values_split)
    return mixed.astype(jnp.bfloat16).reshape(queries.shape)

def mod_block(tokens, pick_list, gain_vec, gate_vec, w_q, w_k, w_v, w_o):
    picked = jnp.take(tokens, pick_list, axis=0)
    gates = jax.nn.sigmoid(jnp.dot(picked, gate_vec, preferred_element_type=jnp.float32))
    normed = rms_norm(picked, gain_vec)
    queries = apply_rope(jnp.dot(normed, w_q, preferred_element_type=jnp.float32), pick_list).astype(jnp.bfloat16)
    keys_rot = apply_rope(jnp.dot(normed, w_k, preferred_element_type=jnp.float32), pick_list).astype(jnp.bfloat16)
    values_out = jnp.dot(normed, w_v, preferred_element_type=jnp.float32).astype(jnp.bfloat16)
    attended = attend(queries, keys_rot, values_out, pick_list, pick_list)
    group_cols = w_o.shape[1] // N_SEQ
    grouped = attended.astype(jnp.float32).reshape(attended.shape[0], N_SEQ, group_cols)
    out_grouped = w_o.astype(jnp.float32).reshape(w_o.shape[0], N_SEQ, group_cols)
    partials = jnp.einsum('cgk,dgk->gcd', grouped, out_grouped).astype(jnp.bfloat16)
    partials = lax.optimization_barrier(partials)
    delta = lax.optimization_barrier(jnp.sum(partials.astype(jnp.float32), axis=0)).astype(jnp.bfloat16)
    updated = (picked.astype(jnp.float32) + gates[:, None] * delta.astype(jnp.float32)).astype(jnp.bfloat16)
    return tokens.at[pick_list].set(updated)

def reference(incoming, chosen, norm_gain, router, w_query, w_key, w_value, w_out_t):
    arrived = jnp.roll(incoming, 1, axis=0)

    def per_section(section_items):
        seq_block, pick_block, gain_vec, gate_vec, w_q, w_k, w_v, w_o = section_items

        def per_seq(seq_items):
            tokens, pick_list = seq_items
            return mod_block(tokens, pick_list, gain_vec, gate_vec, w_q, w_k, w_v, w_o)
        return lax.map(per_seq, (seq_block, pick_block))
    return lax.map(per_section, (arrived, chosen, norm_gain, router, w_query, w_key, w_value, w_out_t))
```

```python
import jax
import jax.numpy as jnp
from jax import lax
from jax.sharding import PartitionSpec as P

HD = 128


EPSILON = 1e-05
ROPE_BASE = 500000.0
NEG_FILL = -1e30


def shifted(value, axis, steps):
    count = lax.axis_size(axis)
    pairs = [(source, (source + steps) % count) for source in range(count)]
    return lax.ppermute(value, axis, pairs)


def rms_norm(rows_in, gain_vec):
    widened = rows_in.astype(jnp.float32)
    inv_scale = lax.rsqrt(jnp.mean(widened * widened, axis=-1, keepdims=True) + EPSILON)
    return (widened * inv_scale * gain_vec[None, :]).astype(jnp.bfloat16)


def apply_rope(projected, positions):
    half_dim = HD // 2
    inverse_freq = ROPE_BASE ** (-2.0 * jnp.arange(half_dim, dtype=jnp.float32) / HD)
    angles = positions.astype(jnp.float32)[:, None] * inverse_freq[None, :]
    cosine = jnp.cos(angles)[:, None, :]
    sine_vals = jnp.sin(angles)[:, None, :]
    shaped = projected.reshape(projected.shape[0], -1, HD)
    first_half = shaped[:, :, :half_dim]
    second_half = shaped[:, :, half_dim:]
    rotated = jnp.concatenate(
        [
            first_half * cosine - second_half * sine_vals,
            second_half * cosine + first_half * sine_vals,
        ],
        axis=-1,
    )
    return rotated.reshape(projected.shape)


def attend_rows(joint_proj, positions, key_live, head_width):
    queries = apply_rope(joint_proj[:, :head_width], positions).astype(jnp.bfloat16)
    keys_rot = apply_rope(joint_proj[:, head_width : 2 * head_width], positions).astype(
        jnp.bfloat16
    )
    values_out = joint_proj[:, 2 * head_width :].astype(jnp.bfloat16)
    heads_split = queries.reshape(queries.shape[0], -1, HD)
    keys_split = keys_rot.reshape(keys_rot.shape[0], -1, HD)
    values_split = values_out.reshape(values_out.shape[0], -1, HD)
    scores = jnp.einsum(
        "qhd,khd->hqk", heads_split, keys_split, preferred_element_type=jnp.float32
    ) * HD ** (-0.5)
    allowed = (positions[None, :] <= positions[:, None]) & key_live[None, :]
    scores = jnp.where(allowed[None, :, :], scores, NEG_FILL)
    peak_val = jnp.max(scores, axis=-1, keepdims=True)
    exponent = jnp.exp(scores - peak_val)
    attn_weights = (exponent / jnp.sum(exponent, axis=-1, keepdims=True)).astype(jnp.bfloat16)
    mixed = jnp.einsum(
        "hqk,khd->qhd", attn_weights, values_split, preferred_element_type=jnp.float32
    )
    return mixed.astype(jnp.bfloat16).reshape(queries.shape)


def shard_layout(pick_list, shards, tok_dev):
    owner_of = pick_list // tok_dev
    shard_ids = jnp.arange(shards, dtype=jnp.int32)
    counts = jnp.sum((owner_of[:, None] == shard_ids[None, :]).astype(jnp.int32), axis=0)
    starts = jnp.cumsum(counts) - counts
    return owner_of, counts, starts


def local_slots(pick_list, shards, tok_dev, slot_cap, my_index):
    _, counts, starts = shard_layout(pick_list, shards, tok_dev)
    padded = jnp.concatenate([pick_list, jnp.zeros((slot_cap,), jnp.int32)])
    slot_ids = jnp.arange(slot_cap, dtype=jnp.int32)
    live = slot_ids < counts[my_index]
    mine = lax.dynamic_slice_in_dim(padded, starts[my_index], slot_cap)
    return jnp.where(live, mine - my_index * tok_dev, 0), live


def per_device(incoming, chosen, norm_gain, router, w_query, w_key, w_value, w_out_t):
    shards = lax.axis_size("seq")
    batches = lax.axis_size("dp")
    my_index = lax.axis_index("seq")
    tok_dev = incoming.shape[2]
    width = incoming.shape[3]
    slot_cap = tok_dev // 4
    part_width = w_query.shape[1]
    head_cols = w_query.shape[2]
    next_pick = shifted(chosen, "section", -1)[0, 0]
    send_rows, send_live = local_slots(next_pick, shards, tok_dev, slot_cap, my_index)
    picked_out = jnp.take(incoming[0, 0], send_rows, axis=0)
    picked_out = jnp.where(send_live[:, None], picked_out, jnp.zeros_like(picked_out))
    raw_rows = shifted(picked_out, "section", 1)
    all_picks = lax.all_gather(chosen[:, 0], "dp", axis=0, tiled=True)
    raw_rows, held_incoming = lax.optimization_barrier((raw_rows, incoming))
    tokens = shifted(held_incoming, "section", 1)[0, 0]
    pick_list = chosen[0, 0]
    chosen_count = pick_list.shape[0]
    local_rows, my_live = local_slots(pick_list, shards, tok_dev, slot_cap, my_index)
    router_gate = jax.nn.sigmoid(jnp.dot(raw_rows, router[0], preferred_element_type=jnp.float32))
    normed = rms_norm(raw_rows, norm_gain[0])
    by_part = normed.reshape(slot_cap, batches, part_width).transpose(1, 0, 2)
    to_all = jnp.broadcast_to(by_part[:, None], (batches, shards, slot_cap, part_width))
    spread = lax.all_to_all(
        to_all.reshape(batches * shards * slot_cap, part_width),
        ("dp", "seq"), split_axis=0, concat_axis=0, tiled=True,
    )
    owners, counts, starts = jax.vmap(lambda p: shard_layout(p, shards, tok_dev))(all_picks)
    slot_of = jnp.arange(chosen_count, dtype=jnp.int32)[None] - jnp.take_along_axis(
        starts, owners, axis=1
    )
    batch_ids = jnp.arange(batches, dtype=jnp.int32)
    flat_of = (batch_ids[:, None] * shards + owners) * slot_cap + slot_of
    compact = jnp.take(spread, flat_of.reshape(-1), axis=0)
    partials = [
        jnp.dot(compact, w[0], preferred_element_type=jnp.float32).astype(jnp.bfloat16)
        for w in (w_query, w_key, w_value)
    ]
    joint_part = jnp.concatenate(partials, axis=1)
    exchanged = lax.all_to_all(joint_part, "dp", split_axis=0, concat_axis=0, tiled=True)
    joint_proj = jnp.sum(
        exchanged.reshape(batches, chosen_count, 3 * head_cols).astype(jnp.float32), axis=0
    )
    all_live = jnp.ones((chosen_count,), dtype=bool)
    attended = attend_rows(joint_proj, pick_list, all_live, head_cols)
    both = lax.all_gather(attended, "dp", axis=0, tiled=True)
    partial_out = lax.dot_general(
        both, w_out_t[0], (((1,), (1,)), ((), ())), preferred_element_type=jnp.float32
    ).astype(jnp.bfloat16)
    slot_ids = jnp.arange(slot_cap, dtype=jnp.int32)
    back_index = jnp.minimum(starts[:, :, None] + slot_ids, chosen_count - 1)
    back_index = back_index + batch_ids[:, None, None] * chosen_count
    slotted = jnp.take(partial_out, back_index.reshape(-1), axis=0)
    returned = lax.all_to_all(slotted, ("dp", "seq"), split_axis=0, concat_axis=0, tiled=True)
    returned = returned.reshape(batches, shards, slot_cap, part_width).astype(jnp.float32)
    delta_rows = jnp.sum(returned, axis=1).transpose(1, 0, 2).reshape(slot_cap, width)
    delta_rows = delta_rows.astype(jnp.bfloat16).astype(jnp.float32)
    updated = (raw_rows.astype(jnp.float32) + router_gate[:, None] * delta_rows).astype(
        jnp.bfloat16
    )
    target = jnp.where(my_live, local_rows, tok_dev)
    result = tokens.at[target].set(updated, mode="drop")
    return result[None, None]


def solution(mesh):
    in_specs = (
        P("section", "dp", "seq", None),
        P("section", "dp", None),
        P("section", None),
        P("section", None),
        P("section", "dp", "seq"),
        P("section", "dp", "seq"),
        P("section", "dp", "seq"),
        P("section", "dp", "seq"),
    )
    out_specs = P("section", "dp", "seq", None)
    return jax.shard_map(
        per_device, mesh=mesh, in_specs=in_specs, out_specs=out_specs, check_vma=False
    )
```

```python
import functools

import jax
import jax.numpy as jnp
import numpy as np
from jax import lax
from jax.experimental import pallas as pl
from jax.experimental.pallas import tpu as pltpu
from jax.sharding import PartitionSpec as P

HD = 128


EPSILON = 1e-05
ROPE_BASE = 500000.0
NEG_FILL = -1e30
MESH = pl.DeviceIdType.MESH
F32 = jnp.float32
BF16 = jnp.bfloat16


def nt_dot(lhs, rhs):
    return lax.dot_general(lhs, rhs, (((1,), (1,)), ((), ())), preferred_element_type=F32)


def nn_dot(lhs, rhs):
    return jnp.dot(lhs, rhs, preferred_element_type=F32)


def ones_where(mask):
    return jnp.where(mask, 1.0, 0.0).astype(BF16)


def iota_f32(shape, dim):
    return lax.broadcasted_iota(jnp.int32, shape, dim).astype(F32)


def as_column(row):
    count = row.shape[1]
    eye = lax.broadcasted_iota(jnp.int32, (count, count), 0) == lax.broadcasted_iota(
        jnp.int32, (count, count), 1
    )
    return jnp.sum(jnp.where(eye, row, 0.0), axis=1, keepdims=True)


def count_below(picks, bound):
    return jnp.sum(jnp.where(picks < bound, 1.0, 0.0), axis=1, keepdims=True)


def local_onehots(picks, lowest, slots, tok_dev):
    count = picks.shape[1]
    mine = (picks >= lowest) & (picks < lowest + tok_dev)
    slot = iota_f32((1, count), 1) - count_below(picks, lowest)
    slot = jnp.where(mine, slot, -1.0)
    by_slot = ones_where(slot == iota_f32((slots, count), 0))
    by_row = ones_where((picks - lowest).astype(F32) == iota_f32((tok_dev, count), 0))
    return by_slot, by_row


def flat_slots(picks, shards, slots, tok_dev):
    count = picks.shape[1]
    order = iota_f32((1, count), 1)
    flat = jnp.zeros((1, count), F32)
    for owner in range(shards):
        low = owner * tok_dev
        inside = (picks >= low) & (picks < low + tok_dev)
        flat = jnp.where(inside, owner * slots + order - count_below(picks, low), flat)
    return flat


def kernel(
    sections, batches, shards,
    tokens, chosen, gain, router, freq, w_q, w_k, w_v, w_o,
    out,
    w_in, w_back, picks, next_pick, picked, raw_rows, arrived, normed, spread,
    compact, part, joint, attended, both, slot_att, out_part, returned,
    w_sem, pick_send, pick_recv, row_send, row_recv, sp_send, sp_recv,
    jt_send, jt_recv, at_send, at_recv, rt_send, rt_recv,
):
    z, g, t = lax.axis_index("section"), lax.axis_index("dp"), lax.axis_index("seq")
    plane = batches * shards
    me = g * shards + t
    after = (lax.rem(z + 1, sections), g, t)
    before = (lax.rem(z + sections - 1, sections), g, t)
    tok_dev, width = tokens.shape
    count = chosen.shape[1]
    slots = tok_dev // 4
    depth, head_cols = w_q.shape

    loads = [
        pltpu.make_async_copy(w, w_in.at[i], w_sem.at[i]) for i, w in enumerate((w_q, w_k, w_v))
    ]
    loads.append(pltpu.make_async_copy(w_o, w_back, w_sem.at[3]))
    for load in loads:
        load.start()

    def peer(step):
        index = lax.rem(me + step, plane)
        return index, (z, lax.div(index, shards), lax.rem(index, shards))

    def mate(step):
        index = lax.rem(g + step, batches)
        return index, (z, index, t)

    def remote(src, dst, send, recv, device):
        return pltpu.make_async_remote_copy(
            src_ref=src, dst_ref=dst, send_sem=send, recv_sem=recv,
            device_id=device, device_id_type=MESH,
        )

    barrier = pltpu.get_barrier_semaphore()
    for device in (after, before):
        pl.semaphore_signal(barrier, inc=1, device_id=device, device_id_type=MESH)

    @pl.loop(1, plane)
    def _(step):
        pl.semaphore_signal(barrier, inc=1, device_id=peer(step)[1], device_id_type=MESH)

    my_picks = chosen[...]
    pick_cols = picks.shape[2]
    padded = my_picks
    if pick_cols > count:
        padded = jnp.concatenate(
            [my_picks, jnp.zeros((1, pick_cols - count), jnp.int32)], axis=1
        )
    picks[g] = jnp.broadcast_to(padded, (8, pick_cols))
    pl.semaphore_wait(barrier, plane + 1)

    pick_back = remote(
        picks.at[g], next_pick, pick_send.at[0], pick_recv.at[batches], before
    )
    pick_back.start()

    def pick_copy(step):
        index, device = mate(step)
        return remote(picks.at[g], picks.at[g], pick_send.at[step], pick_recv.at[g], device)

    for step in range(1, batches):
        pick_copy(step).start()

    pick_back.wait_recv()
    lowest = t * tok_dev
    by_slot, by_row = local_onehots(next_pick[0:1, :count], lowest, slots, tok_dev)
    gather = nt_dot(by_slot, by_row).astype(BF16)
    picked[...] = nn_dot(gather, tokens[...]).astype(BF16)
    row_copy = remote(picked, raw_rows, row_send.at[0], row_recv.at[0], after)
    row_copy.start()

    angles = as_column(my_picks.astype(F32)) * freq[...]
    cosine = jnp.cos(angles)
    lane = lax.broadcasted_iota(jnp.int32, (count, HD), 1)
    sine = jnp.where(lane < HD // 2, -1.0, 1.0) * jnp.sin(angles)

    row_copy.wait_recv()
    relay = remote(tokens, arrived, row_send.at[1], row_recv.at[1], after)
    relay.start()
    rows = raw_rows[...].astype(F32)
    inv_scale = lax.rsqrt(jnp.mean(rows * rows, axis=1, keepdims=True) + EPSILON)
    scaled = (rows * inv_scale * gain[...]).astype(BF16)
    for b in range(batches):
        normed[b] = scaled[:, b * depth : (b + 1) * depth]

    def spread_copy(step):
        index, device = peer(step)
        return remote(
            normed.at[lax.div(index, shards)], spread.at[me],
            sp_send.at[index], sp_recv.at[me], device,
        )

    @pl.loop(1, plane)
    def _(step):
        spread_copy(step).start()

    spread[me] = normed[g]
    gate = jax.nn.sigmoid(
        jnp.sum(rows * router[...].astype(F32), axis=1, keepdims=True)
    )

    def arrived_from(buffer, sems, index):
        remote(buffer.at[index], buffer.at[index], sems.at[index], sems.at[index], after).wait_recv()

    for step in range(1, batches):
        arrived_from(picks, pick_recv, mate(step)[0])
    flats = [flat_slots(picks[b, 0:1, :count], shards, slots, tok_dev) for b in range(batches)]
    flat_cols = [as_column(flat) for flat in flats]

    @pl.loop(1, plane)
    def _(step):
        arrived_from(spread, sp_recv, peer(step)[0])

    for b in range(batches):
        choose = ones_where(flat_cols[b] == iota_f32((count, shards * slots), 1))
        source = spread[b * shards : (b + 1) * shards].reshape(shards * slots, depth)
        compact[b * count : (b + 1) * count, :] = nn_dot(choose, source).astype(BF16)

    cols = min(256, head_cols)

    def joint_copy(step, which):
        index, device = mate(step)
        return remote(
            part.at[index, which], joint.at[g, which],
            jt_send.at[step, which], jt_recv.at[g, which], device,
        )

    for which in range(3):
        loads[which].wait()

        @pl.loop(0, head_cols // cols)
        def _(block):
            at = pl.ds(pl.multiple_of(block * cols, cols), cols)
            product = nn_dot(compact[...], w_in[which, :, at]).astype(BF16)
            for b in range(batches):
                part[b, which, :, at] = product[b * count : (b + 1) * count]

        for step in range(1, batches):
            joint_copy(step, which).start()
        joint[g, which] = part[g, which]

    summed = []
    for which in range(3):
        for step in range(1, batches):
            index = mate(step)[0]
            slot = joint.at[index, which]
            remote(
                slot, slot, jt_recv.at[index, which], jt_recv.at[index, which], after
            ).wait_recv()
        total = joint[0, which].astype(F32)
        for b in range(1, batches):
            total = total + joint[b, which].astype(F32)
        summed.append(total)

    def rope(value):
        swapped = jnp.concatenate([value[:, HD // 2 :], value[:, : HD // 2]], axis=1)
        return (value * cosine + swapped * sine).astype(BF16)

    causal = lax.broadcasted_iota(jnp.int32, (count, count), 1) <= lax.broadcasted_iota(
        jnp.int32, (count, count), 0
    )
    for head in range(head_cols // HD):
        at = slice(head * HD, (head + 1) * HD)
        scores = nt_dot(rope(summed[0][:, at]), rope(summed[1][:, at])) * HD ** (-0.5)
        scores = jnp.where(causal, scores, NEG_FILL)
        exponent = jnp.exp(scores - jnp.max(scores, axis=1, keepdims=True))
        weights = (exponent / jnp.sum(exponent, axis=1, keepdims=True)).astype(BF16)
        attended[:, at] = nn_dot(weights, summed[2][:, at].astype(BF16)).astype(BF16)

    def attended_copy(step):
        index, device = mate(step)
        return remote(attended, both.at[g], at_send.at[step], at_recv.at[g], device)

    for step in range(1, batches):
        attended_copy(step).start()
    both[g] = attended[...]
    loads[3].wait()

    def return_copy(index):
        device = (z, lax.div(index, shards), lax.rem(index, shards))
        return remote(
            out_part.at[index], returned.at[me], rt_send.at[index], rt_recv.at[me], device
        )

    out_cols = min(256, depth)
    for step in range(batches):
        batch = mate(step)[0]
        if step:
            arrived_from(both, at_recv, batch)
        place = flat_slots(picks[batch, 0:1, :count], shards, slots, tok_dev)
        place = ones_where(place == iota_f32((shards * slots, count), 0))
        slot_att[...] = nn_dot(place, both[batch]).astype(BF16)

        @pl.loop(0, depth // out_cols)
        def _(block):
            start = pl.multiple_of(block * out_cols, out_cols)
            at = pl.ds(start, out_cols)
            product = nt_dot(slot_att[...], w_back[at, :]).astype(BF16)
            for owner in range(shards):
                out_part[batch * shards + owner, :, at] = product[
                    owner * slots : (owner + 1) * slots
                ]

        @pl.loop(1 if step == 0 else 0, shards)
        def _(turn):
            return_copy(batch * shards + lax.rem(t + turn, shards)).start()

    returned[me] = out_part[me]
    by_slot, by_row = local_onehots(my_picks, lowest, slots, tok_dev)
    scatter = nt_dot(by_row, by_slot).astype(BF16)
    held = jnp.sum(by_row.astype(F32), axis=1, keepdims=True) > 0.5
    relay.wait_recv()

    @pl.loop(1, plane)
    def _(step):
        arrived_from(returned, rt_recv, peer(step)[0])

    for b in range(batches):
        at = slice(b * depth, (b + 1) * depth)
        delta = returned[b * shards].astype(F32)
        for owner in range(1, shards):
            delta = delta + returned[b * shards + owner].astype(F32)
        delta = delta.astype(BF16).astype(F32)
        updated = (raw_rows[:, at].astype(F32) + gate * delta).astype(BF16)
        replaced = nn_dot(scatter, updated)
        out[:, at] = jnp.where(held, replaced, arrived[:, at].astype(F32)).astype(BF16)

    pick_back.wait_send()
    row_copy.wait_send()
    relay.wait_send()
    for step in range(1, batches):
        pick_copy(step).wait_send()
        attended_copy(step).wait_send()
        for which in range(3):
            joint_copy(step, which).wait_send()

    @pl.loop(1, plane)
    def _(step):
        spread_copy(step).wait_send()
        return_copy(peer(step)[0]).wait_send()


def per_device(incoming, chosen, norm_gain, router, w_query, w_key, w_value, w_out_t):
    sections = lax.axis_size("section")
    batches = lax.axis_size("dp")
    shards = lax.axis_size("seq")
    plane = batches * shards
    tok_dev, width = incoming.shape[2:]
    count = chosen.shape[2]
    slots = tok_dev // 4
    depth, head_cols = w_query.shape[1:]
    half = np.arange(HD // 2, dtype=np.float32)
    freq = np.float32(ROPE_BASE) ** (np.float32(-2.0) * half / np.float32(HD))
    freq = jnp.asarray(np.concatenate([freq, freq])[None].astype(np.float32))
    pick_cols = -(-count // 128) * 128
    vmem = pl.BlockSpec(memory_space=pltpu.VMEM)
    hbm = pl.BlockSpec(memory_space=pl.ANY)
    dma = pltpu.SemaphoreType.DMA
    result = pl.pallas_call(
        functools.partial(kernel, sections, batches, shards),
        out_shape=jax.ShapeDtypeStruct((tok_dev, width), BF16),
        in_specs=[vmem] * 5 + [hbm] * 4,
        out_specs=vmem,
        scratch_shapes=[
            pltpu.VMEM((3, depth, head_cols), BF16),
            pltpu.VMEM((depth, head_cols), BF16),
            pltpu.VMEM((batches, 8, pick_cols), jnp.int32),
            pltpu.VMEM((8, pick_cols), jnp.int32),
            pltpu.VMEM((slots, width), BF16),
            pltpu.VMEM((slots, width), BF16),
            pltpu.VMEM((tok_dev, width), BF16),
            pltpu.VMEM((batches, slots, depth), BF16),
            pltpu.VMEM((plane, slots, depth), BF16),
            pltpu.VMEM((batches * count, depth), BF16),
            pltpu.VMEM((batches, 3, count, head_cols), BF16),
            pltpu.VMEM((batches, 3, count, head_cols), BF16),
            pltpu.VMEM((count, head_cols), BF16),
            pltpu.VMEM((batches, count, head_cols), BF16),
            pltpu.VMEM((shards * slots, head_cols), BF16),
            pltpu.VMEM((plane, slots, depth), BF16),
            pltpu.VMEM((plane, slots, depth), BF16),
            dma((4,)),
            dma((batches,)), dma((batches + 1,)),
            dma((2,)), dma((2,)),
            dma((plane,)), dma((plane,)),
            dma((batches, 3)), dma((batches, 3)),
            dma((batches,)), dma((batches,)),
            dma((plane,)), dma((plane,)),
        ],
        compiler_params=pltpu.CompilerParams(
            collective_id=0, has_side_effects=True, vmem_limit_bytes=52 * 1024 * 1024
        ),
    )(
        incoming[0, 0], chosen[0], norm_gain, router, freq,
        w_query[0], w_key[0], w_value[0], w_out_t[0],
    )
    return result[None, None]


def solution(mesh):
    in_specs = (
        P("section", "dp", "seq", None),
        P("section", "dp", None),
        P("section", None),
        P("section", None),
        P("section", "dp", "seq"),
        P("section", "dp", "seq"),
        P("section", "dp", "seq"),
        P("section", "dp", "seq"),
    )
    out_specs = P("section", "dp", "seq", None)
    return jax.shard_map(
        per_device, mesh=mesh, in_specs=in_specs, out_specs=out_specs, check_vma=False
    )
```

```python
import functools

import jax
import jax.numpy as jnp
import numpy as np
from jax import lax
from jax.experimental import pallas as pl
from jax.experimental.pallas import tpu as pltpu
from jax.sharding import PartitionSpec as P

HD = 128


EPSILON = 1e-05
ROPE_BASE = 500000.0
NEG_FILL = -1e30
MESH = pl.DeviceIdType.MESH
F32 = jnp.float32
BF16 = jnp.bfloat16


def nt_dot(lhs, rhs):
    return lax.dot_general(lhs, rhs, (((1,), (1,)), ((), ())), preferred_element_type=F32)


def nn_dot(lhs, rhs):
    return jnp.dot(lhs, rhs, preferred_element_type=F32)


def ones_where(mask):
    return jnp.where(mask, 1.0, 0.0).astype(BF16)


def iota_f32(shape, dim):
    return lax.broadcasted_iota(jnp.int32, shape, dim).astype(F32)


def as_column(row):
    count = row.shape[1]
    eye = lax.broadcasted_iota(jnp.int32, (count, count), 0) == lax.broadcasted_iota(
        jnp.int32, (count, count), 1
    )
    return jnp.sum(jnp.where(eye, row, 0.0), axis=1, keepdims=True)


def count_below(picks, bound):
    return jnp.sum(jnp.where(picks < bound, 1.0, 0.0), axis=1, keepdims=True)


def local_onehots(picks, lowest, slots, tok_dev):
    count = picks.shape[1]
    mine = (picks >= lowest) & (picks < lowest + tok_dev)
    slot = iota_f32((1, count), 1) - count_below(picks, lowest)
    slot = jnp.where(mine, slot, -1.0)
    by_slot = ones_where(slot == iota_f32((slots, count), 0))
    by_row = ones_where((picks - lowest).astype(F32) == iota_f32((tok_dev, count), 0))
    return by_slot, by_row


def flat_slots(picks, shards, slots, tok_dev):
    count = picks.shape[1]
    order = iota_f32((1, count), 1)
    flat = jnp.zeros((1, count), F32)
    for owner in range(shards):
        low = owner * tok_dev
        inside = (picks >= low) & (picks < low + tok_dev)
        flat = jnp.where(inside, owner * slots + order - count_below(picks, low), flat)
    return flat


def kernel(
    sections, batches, shards,
    tokens_hbm, chosen_hbm, gain_hbm, router, w_q, w_k, w_v, w_o,
    out,
    tokens, chosen, gain, w_in, w_back, inverse, inverse_in, picks, next_pick, picked, raw_rows, arrived, normed, spread,
    compact, part, joint, attended, both, slot_att, out_part, middle, returned,
    w_sem, pick_send, pick_recv, row_send, row_recv, sp_send, sp_recv,
    fw_send, jt_send, jt_recv, at_send, at_recv, md_send, md_recv, rt_send, rt_recv,
):
    z, g, t = lax.axis_index("section"), lax.axis_index("dp"), lax.axis_index("seq")
    plane = batches * shards
    me = g * shards + t
    pair = 2 if shards % 2 == 0 else 1
    rows_of = shards // pair
    core, row = lax.rem(t, pair), lax.div(t, pair)
    sibling = (z, g, row * pair + lax.rem(core + 1, pair))
    after = (lax.rem(z + 1, sections), g, t)
    before = (lax.rem(z + sections - 1, sections), g, t)
    tok_dev, width = tokens.shape
    count = chosen.shape[1]
    slots = tok_dev // 4
    depth, head_cols = w_q.shape

    loads = [
        pltpu.make_async_copy(w, w_in.at[i], w_sem.at[i]) for i, w in enumerate((w_q, w_k, w_v))
    ]
    loads.append(pltpu.make_async_copy(w_o, w_back, w_sem.at[3]))
    early = [
        pltpu.make_async_copy(chosen_hbm, chosen, w_sem.at[4]),
        pltpu.make_async_copy(tokens_hbm, tokens, w_sem.at[5]),
        pltpu.make_async_copy(gain_hbm, gain, w_sem.at[6]),
    ]
    for load in early + loads:
        load.start()

    def peer(step):
        index = lax.rem(me + step, plane)
        return index, (z, lax.div(index, shards), lax.rem(index, shards))

    def mate(step):
        index = lax.rem(g + step, batches)
        return index, (z, index, t)

    def remote(src, dst, send, recv, device):
        return pltpu.make_async_remote_copy(
            src_ref=src, dst_ref=dst, send_sem=send, recv_sem=recv,
            device_id=device, device_id_type=MESH,
        )

    barrier = pltpu.get_barrier_semaphore()
    for device in (after, before):
        pl.semaphore_signal(barrier, inc=1, device_id=device, device_id_type=MESH)

    @pl.loop(1, plane)
    def _(step):
        pl.semaphore_signal(barrier, inc=1, device_id=peer(step)[1], device_id_type=MESH)

    early[0].wait()
    my_picks = chosen[...]
    pick_cols = picks.shape[2]
    padded = my_picks
    if pick_cols > count:
        padded = jnp.concatenate(
            [my_picks, jnp.zeros((1, pick_cols - count), jnp.int32)], axis=1
        )
    picks[g] = jnp.broadcast_to(padded, (8, pick_cols))
    pl.semaphore_wait(barrier, plane + 1)

    pick_back = remote(
        picks.at[g], next_pick, pick_send.at[0], pick_recv.at[batches], before
    )
    pick_back.start()

    def pick_copy(step):
        index, device = mate(step)
        return remote(picks.at[g], picks.at[g], pick_send.at[step], pick_recv.at[g], device)

    for step in range(1, batches):
        pick_copy(step).start()

    pick_back.wait_recv()
    lowest = t * tok_dev
    by_slot, by_row = local_onehots(next_pick[0:1, :count], lowest, slots, tok_dev)
    gather = nt_dot(by_slot, by_row).astype(BF16)
    early[1].wait()
    chosen_rows = nn_dot(gather, tokens[...])
    inverse[...] = jnp.broadcast_to(
        lax.rsqrt(jnp.mean(chosen_rows * chosen_rows, axis=1, keepdims=True) + EPSILON),
        inverse.shape,
    )
    inverse_copy = remote(
        inverse, inverse_in, row_send.at[batches + 1], row_recv.at[batches + 1], after
    )
    inverse_copy.start()
    for b in range(batches):
        picked[b] = chosen_rows[:, b * depth : (b + 1) * depth].astype(BF16)

    def row_copy(step):
        b = mate(step)[0]
        return remote(picked.at[b], raw_rows.at[b], row_send.at[step], row_recv.at[step], after)

    order = [step % batches for step in range(1, batches + 1)]
    for step in order:
        row_copy(step).start()

    lane = lax.broadcasted_iota(jnp.int32, (count, HD), 1)
    twin = jnp.where(lane < HD // 2, lane, lane - HD // 2).astype(F32)
    angles = as_column(my_picks.astype(F32)) * jnp.exp(twin * (-2.0 / HD * np.log(ROPE_BASE)))
    cosine = jnp.cos(angles)
    sine = jnp.where(lane < HD // 2, -1.0, 1.0) * jnp.sin(angles)
    early[2].wait()

    def spread_copy(step, turn):
        b = mate(step)[0]
        far = lax.rem(row + turn, rows_of)
        return remote(
            normed.at[b], spread.at[me], sp_send.at[b * rows_of + far], sp_recv.at[me],
            (z, b, far * pair + core),
        )

    def forward_copy(source):
        return remote(
            spread.at[source], spread.at[source], fw_send.at[source], sp_recv.at[source], sibling
        )

    inverse_copy.wait_recv()
    inv_scale = inverse_in[:, 0:1]
    for step in order:
        row_copy(step).wait_recv()
        b = mate(step)[0]
        at = pl.ds(pl.multiple_of(b * depth, 128), depth)
        normed[b] = (raw_rows[b].astype(F32) * inv_scale * gain[:, at]).astype(BF16)
        if step == 0:
            spread[me] = normed[g]
            if pair == 2:
                forward_copy(me).start()

        @pl.loop(1 if step == 0 else 0, rows_of)
        def _(turn):
            spread_copy(step, turn).start()

    relay = remote(tokens, arrived, row_send.at[batches], row_recv.at[batches], after)
    relay.start()
    logits = jnp.zeros((slots, 1), F32)
    for b in range(batches):
        logits = logits + jnp.sum(
            raw_rows[b].astype(F32) * router[:, b * depth : (b + 1) * depth].astype(F32),
            axis=1, keepdims=True,
        )
    gate = jax.nn.sigmoid(logits)

    def arrived_from(buffer, sems, index):
        remote(buffer.at[index], buffer.at[index], sems.at[index], sems.at[index], after).wait_recv()

    for step in range(1, batches):
        arrived_from(picks, pick_recv, mate(step)[0])
    flats = [flat_slots(picks[b, 0:1, :count], shards, slots, tok_dev) for b in range(batches)]
    flat_cols = [as_column(flat) for flat in flats]

    half = batches * rows_of

    def same_core(step):
        index = lax.rem(g * rows_of + row + step, half)
        return lax.div(index, rows_of), lax.rem(index, rows_of)

    @pl.loop(1, half)
    def _(step):
        b, far = same_core(step)
        source = b * shards + far * pair + core
        arrived_from(spread, sp_recv, source)
        if pair == 2:
            forward_copy(source).start()

    if pair == 2:

        @pl.loop(0, half)
        def _(step):
            b, far = same_core(step)
            arrived_from(spread, sp_recv, b * shards + far * pair + 1 - core)

    for b in range(batches):
        choose = ones_where(flat_cols[b] == iota_f32((count, shards * slots), 1))
        source = spread[b * shards : (b + 1) * shards].reshape(shards * slots, depth)
        compact[b * count : (b + 1) * count, :] = nn_dot(choose, source).astype(BF16)

    cols = min(256, head_cols)

    def joint_copy(step, which):
        index, device = mate(step)
        return remote(
            part.at[index, which], joint.at[g, which],
            jt_send.at[step, which], jt_recv.at[g, which], device,
        )

    for which in range(3):
        loads[which].wait()

        @pl.loop(0, head_cols // cols)
        def _(block):
            at = pl.ds(pl.multiple_of(block * cols, cols), cols)
            product = nn_dot(compact[...], w_in[which, :, at]).astype(BF16)
            for b in range(batches):
                part[b, which, :, at] = product[b * count : (b + 1) * count]

        for step in range(1, batches):
            joint_copy(step, which).start()
        joint[g, which] = part[g, which]

    summed = []
    for which in range(3):
        for step in range(1, batches):
            index = mate(step)[0]
            slot = joint.at[index, which]
            remote(
                slot, slot, jt_recv.at[index, which], jt_recv.at[index, which], after
            ).wait_recv()
        total = joint[0, which].astype(F32)
        for b in range(1, batches):
            total = total + joint[b, which].astype(F32)
        summed.append(total)

    def rope(value):
        swapped = jnp.concatenate([value[:, HD // 2 :], value[:, : HD // 2]], axis=1)
        return (value * cosine + swapped * sine).astype(BF16)

    causal = lax.broadcasted_iota(jnp.int32, (count, count), 1) <= lax.broadcasted_iota(
        jnp.int32, (count, count), 0
    )
    for head in range(head_cols // HD):
        at = slice(head * HD, (head + 1) * HD)
        scores = nt_dot(rope(summed[0][:, at]), rope(summed[1][:, at])) * HD ** (-0.5)
        scores = jnp.where(causal, scores, NEG_FILL)
        exponent = jnp.exp(scores - jnp.max(scores, axis=1, keepdims=True))
        weights = (exponent / jnp.sum(exponent, axis=1, keepdims=True)).astype(BF16)
        attended[:, at] = nn_dot(weights, summed[2][:, at].astype(BF16)).astype(BF16)

    def attended_copy(step):
        index, device = mate(step)
        return remote(attended, both.at[g], at_send.at[step], at_recv.at[g], device)

    for step in range(1, batches):
        attended_copy(step).start()
    both[g] = attended[...]
    loads[3].wait()

    def middle_copy(batch, far):
        index = batch * shards + far * pair + 1 - core
        slot = batch * rows_of + far
        return remote(
            out_part.at[index], middle.at[slot], md_send.at[slot], md_recv.at[slot], sibling
        )

    def return_copy(batch, far):
        place = far * pair + core
        return remote(
            out_part.at[batch * shards + place], returned.at[g * rows_of + row],
            rt_send.at[batch * rows_of + far], rt_recv.at[g * rows_of + row], (z, batch, place),
        )

    def send_sums(step):
        batch = mate(step)[0]

        @pl.loop(0, rows_of)
        def _(turn):
            far = lax.rem(row + 1 + turn, rows_of)
            index = batch * shards + far * pair + core
            if pair == 2:
                arrived_from(middle, md_recv, batch * rows_of + far)
                out_part[index] = (
                    out_part[index].astype(F32) + middle[batch * rows_of + far].astype(F32)
                ).astype(BF16)
            if step:
                return_copy(batch, far).start()
            else:

                @pl.when(turn < rows_of - 1)
                def _():
                    return_copy(batch, far).start()

    out_cols = min(256, depth)
    for step in range(batches):
        batch = mate(step)[0]
        if step:
            arrived_from(both, at_recv, batch)
        place = flat_slots(picks[batch, 0:1, :count], shards, slots, tok_dev)
        place = ones_where(place == iota_f32((shards * slots, count), 0))
        slot_att[...] = nn_dot(place, both[batch]).astype(BF16)

        @pl.loop(0, depth // out_cols)
        def _(block):
            start = pl.multiple_of(block * out_cols, out_cols)
            at = pl.ds(start, out_cols)
            product = nt_dot(slot_att[...], w_back[at, :]).astype(BF16)
            for owner in range(shards):
                out_part[batch * shards + owner, :, at] = product[
                    owner * slots : (owner + 1) * slots
                ]

        if pair == 2:

            @pl.loop(0, rows_of)
            def _(turn):
                middle_copy(batch, lax.rem(row + 1 + turn, rows_of)).start()

        if step:
            send_sums(step - 1)
    send_sums(batches - 1)
    returned[g * rows_of + row] = out_part[me]
    by_slot, by_row = local_onehots(my_picks, lowest, slots, tok_dev)
    scatter = nt_dot(by_row, by_slot).astype(BF16)
    held = jnp.sum(by_row.astype(F32), axis=1, keepdims=True) > 0.5
    relay.wait_recv()

    @pl.loop(1, half)
    def _(step):
        b, far = same_core(step)
        arrived_from(returned, rt_recv, b * rows_of + far)

    for b in range(batches):
        at = slice(b * depth, (b + 1) * depth)
        delta = returned[b * rows_of].astype(F32)
        for far in range(1, rows_of):
            delta = delta + returned[b * rows_of + far].astype(F32)
        delta = delta.astype(BF16).astype(F32)
        updated = (raw_rows[b].astype(F32) + gate * delta).astype(BF16)
        replaced = nn_dot(scatter, updated)
        out[:, at] = jnp.where(held, replaced, arrived[:, at].astype(F32)).astype(BF16)

    pick_back.wait_send()
    inverse_copy.wait_send()
    relay.wait_send()
    for step in range(batches):
        row_copy(step).wait_send()

        @pl.loop(1 if step == 0 else 0, rows_of)
        def _(turn):
            spread_copy(step, turn).wait_send()
            return_copy(mate(step)[0], lax.rem(row + turn, rows_of)).wait_send()

    for step in range(1, batches):
        pick_copy(step).wait_send()
        attended_copy(step).wait_send()
        for which in range(3):
            joint_copy(step, which).wait_send()

    if pair == 2:

        @pl.loop(0, half)
        def _(step):
            b, far = same_core(step)
            forward_copy(b * shards + far * pair + core).wait_send()
            middle_copy(b, far).wait_send()


def per_device(incoming, chosen, norm_gain, router, w_query, w_key, w_value, w_out_t):
    sections = lax.axis_size("section")
    batches = lax.axis_size("dp")
    shards = lax.axis_size("seq")
    plane = batches * shards
    tok_dev, width = incoming.shape[2:]
    count = chosen.shape[2]
    slots = tok_dev // 4
    depth, head_cols = w_query.shape[1:]
    pair = 2 if shards % 2 == 0 else 1
    half = batches * (shards // pair)
    pick_cols = -(-count // 128) * 128
    vmem = pl.BlockSpec(memory_space=pltpu.VMEM)
    hbm = pl.BlockSpec(memory_space=pl.ANY)
    dma = pltpu.SemaphoreType.DMA
    result = pl.pallas_call(
        functools.partial(kernel, sections, batches, shards),
        out_shape=jax.ShapeDtypeStruct((tok_dev, width), BF16),
        in_specs=[hbm] * 3 + [vmem] + [hbm] * 4,
        out_specs=vmem,
        scratch_shapes=[
            pltpu.VMEM((tok_dev, width), BF16),
            pltpu.VMEM((1, count), jnp.int32),
            pltpu.VMEM((1, width), F32),
            pltpu.VMEM((3, depth, head_cols), BF16),
            pltpu.VMEM((depth, head_cols), BF16),
            pltpu.VMEM((slots, 128), F32),
            pltpu.VMEM((slots, 128), F32),
            pltpu.VMEM((batches, 8, pick_cols), jnp.int32),
            pltpu.VMEM((8, pick_cols), jnp.int32),
            pltpu.VMEM((batches, slots, depth), BF16),
            pltpu.VMEM((batches, slots, depth), BF16),
            pltpu.VMEM((tok_dev, width), BF16),
            pltpu.VMEM((batches, slots, depth), BF16),
            pltpu.VMEM((plane, slots, depth), BF16),
            pltpu.VMEM((batches * count, depth), BF16),
            pltpu.VMEM((batches, 3, count, head_cols), BF16),
            pltpu.VMEM((batches, 3, count, head_cols), BF16),
            pltpu.VMEM((count, head_cols), BF16),
            pltpu.VMEM((batches, count, head_cols), BF16),
            pltpu.VMEM((shards * slots, head_cols), BF16),
            pltpu.VMEM((plane, slots, depth), BF16),
            pltpu.VMEM((half, slots, depth), BF16),
            pltpu.VMEM((half, slots, depth), BF16),
            dma((7,)),
            dma((batches,)), dma((batches + 1,)),
            dma((batches + 2,)), dma((batches + 2,)),
            dma((half,)), dma((plane,)), dma((plane,)),
            dma((batches, 3)), dma((batches, 3)),
            dma((batches,)), dma((batches,)),
            dma((half,)), dma((half,)), dma((half,)), dma((half,)),
        ],
        compiler_params=pltpu.CompilerParams(
            collective_id=0, has_side_effects=True, vmem_limit_bytes=52 * 1024 * 1024
        ),
    )(
        incoming[0, 0], chosen[0], norm_gain, router,
        w_query[0], w_key[0], w_value[0], w_out_t[0],
    )
    return result[None, None]


def solution(mesh):
    in_specs = (
        P("section", "dp", "seq", None),
        P("section", "dp", None),
        P("section", None),
        P("section", None),
        P("section", "dp", "seq"),
        P("section", "dp", "seq"),
        P("section", "dp", "seq"),
        P("section", "dp", "seq"),
    )
    out_specs = P("section", "dp", "seq", None)
    return jax.shard_map(
        per_device, mesh=mesh, in_specs=in_specs, out_specs=out_specs, check_vma=False
    )
```

```python
import functools

import jax
import jax.numpy as jnp
import numpy as np
from jax import lax
from jax.experimental import pallas as pl
from jax.experimental.pallas import tpu as pltpu
from jax.sharding import PartitionSpec as P

HD = 128


EPSILON = 1e-05
ROPE_BASE = 500000.0
NEG_FILL = -1e30
MESH = pl.DeviceIdType.MESH
F32 = jnp.float32
BF16 = jnp.bfloat16


def nt_dot(lhs, rhs):
    return lax.dot_general(lhs, rhs, (((1,), (1,)), ((), ())), preferred_element_type=F32)


def nn_dot(lhs, rhs):
    return jnp.dot(lhs, rhs, preferred_element_type=F32)


def ones_where(mask):
    return jnp.where(mask, 1.0, 0.0).astype(BF16)


def iota_f32(shape, dim):
    return lax.broadcasted_iota(jnp.int32, shape, dim).astype(F32)


def as_column(row):
    count = row.shape[1]
    eye = lax.broadcasted_iota(jnp.int32, (count, count), 0) == lax.broadcasted_iota(
        jnp.int32, (count, count), 1
    )
    return jnp.sum(jnp.where(eye, row, 0.0), axis=1, keepdims=True)


def count_below(picks, bound):
    return jnp.sum(jnp.where(picks < bound, 1.0, 0.0), axis=1, keepdims=True)


def local_onehots(picks, lowest, slots, tok_dev):
    count = picks.shape[1]
    mine = (picks >= lowest) & (picks < lowest + tok_dev)
    slot = iota_f32((1, count), 1) - count_below(picks, lowest)
    slot = jnp.where(mine, slot, -1.0)
    by_slot = ones_where(slot == iota_f32((slots, count), 0))
    by_row = ones_where((picks - lowest).astype(F32) == iota_f32((tok_dev, count), 0))
    return by_slot, by_row


def flat_slots(picks, shards, slots, tok_dev):
    count = picks.shape[1]
    order = iota_f32((1, count), 1)
    flat = jnp.zeros((1, count), F32)
    for owner in range(shards):
        low = owner * tok_dev
        inside = (picks >= low) & (picks < low + tok_dev)
        flat = jnp.where(inside, owner * slots + order - count_below(picks, low), flat)
    return flat


def kernel(
    sections, batches, shards,
    tokens_hbm, chosen_hbm, gain_hbm, router_hbm, w_q, w_k, w_v, w_o,
    out,
    tokens, chosen, gain, router, w_in, w_back, inverse, inverse_in, picks, next_pick, picked, raw_rows, arrived, normed, spread,
    compact, part, joint, attended, both, slot_att, out_part, middle, returned,
    w_sem, pick_send, pick_recv, row_send, row_recv, sp_send, sp_recv,
    fw_send, jt_send, jt_recv, at_send, at_recv, md_send, md_recv, rt_send, rt_recv,
):
    z, g, t = lax.axis_index("section"), lax.axis_index("dp"), lax.axis_index("seq")
    plane = batches * shards
    me = g * shards + t
    pair = 2 if shards % 2 == 0 else 1
    rows_of = shards // pair
    core, row = lax.rem(t, pair), lax.div(t, pair)
    sibling = (z, g, row * pair + lax.rem(core + 1, pair))
    after = (lax.rem(z + 1, sections), g, t)
    before = (lax.rem(z + sections - 1, sections), g, t)
    tok_dev, width = tokens.shape
    count = chosen.shape[1]
    slots = tok_dev // 4
    depth, head_cols = w_q.shape

    loads = [
        pltpu.make_async_copy(w, w_in.at[i], w_sem.at[i]) for i, w in enumerate((w_q, w_k, w_v))
    ]
    loads.append(pltpu.make_async_copy(w_o, w_back, w_sem.at[3]))
    early = [
        pltpu.make_async_copy(chosen_hbm, chosen, w_sem.at[4]),
        pltpu.make_async_copy(tokens_hbm, tokens, w_sem.at[5]),
        pltpu.make_async_copy(gain_hbm, gain, w_sem.at[6]),
        pltpu.make_async_copy(router_hbm, router, w_sem.at[7]),
    ]
    for load in early + loads:
        load.start()

    def peer(step):
        index = lax.rem(me + step, plane)
        return index, (z, lax.div(index, shards), lax.rem(index, shards))

    def mate(step):
        index = lax.rem(g + step, batches)
        return index, (z, index, t)

    def remote(src, dst, send, recv, device):
        return pltpu.make_async_remote_copy(
            src_ref=src, dst_ref=dst, send_sem=send, recv_sem=recv,
            device_id=device, device_id_type=MESH,
        )

    barrier = pltpu.get_barrier_semaphore()
    for device in (after, before):
        pl.semaphore_signal(barrier, inc=1, device_id=device, device_id_type=MESH)

    @pl.loop(1, plane)
    def _(step):
        pl.semaphore_signal(barrier, inc=1, device_id=peer(step)[1], device_id_type=MESH)

    early[0].wait()
    my_picks = chosen[...]
    pick_cols = picks.shape[2]
    padded = my_picks
    if pick_cols > count:
        padded = jnp.concatenate(
            [my_picks, jnp.zeros((1, pick_cols - count), jnp.int32)], axis=1
        )
    picks[g] = jnp.broadcast_to(padded, (8, pick_cols))
    pl.semaphore_wait(barrier, plane + 1)

    pick_back = remote(
        picks.at[g], next_pick, pick_send.at[0], pick_recv.at[batches], before
    )
    pick_back.start()

    def pick_copy(step):
        index, device = mate(step)
        return remote(picks.at[g], picks.at[g], pick_send.at[step], pick_recv.at[g], device)

    for step in range(1, batches):
        pick_copy(step).start()

    pick_back.wait_recv()
    lowest = t * tok_dev
    by_slot, by_row = local_onehots(next_pick[0:1, :count], lowest, slots, tok_dev)
    gather = nt_dot(by_slot, by_row).astype(BF16)
    early[1].wait()
    chosen_rows = nn_dot(gather, tokens[...])
    inverse[...] = jnp.broadcast_to(
        lax.rsqrt(jnp.mean(chosen_rows * chosen_rows, axis=1, keepdims=True) + EPSILON),
        inverse.shape,
    )
    inverse_copy = remote(
        inverse, inverse_in, row_send.at[batches + 1], row_recv.at[batches + 1], after
    )
    inverse_copy.start()
    for b in range(batches):
        picked[b] = chosen_rows[:, b * depth : (b + 1) * depth].astype(BF16)

    def row_copy(step):
        b = mate(step)[0]
        return remote(picked.at[b], raw_rows.at[b], row_send.at[step], row_recv.at[step], after)

    order = [step % batches for step in range(1, batches + 1)]
    for step in order:
        row_copy(step).start()

    lane = lax.broadcasted_iota(jnp.int32, (count, HD), 1)
    twin = jnp.where(lane < HD // 2, lane, lane - HD // 2).astype(F32)
    angles = as_column(my_picks.astype(F32)) * jnp.exp(twin * (-2.0 / HD * np.log(ROPE_BASE)))
    cosine = jnp.cos(angles)
    sine = jnp.where(lane < HD // 2, -1.0, 1.0) * jnp.sin(angles)
    early[2].wait()

    def spread_copy(step, turn):
        b = mate(step)[0]
        far = lax.rem(row + turn, rows_of)
        return remote(
            normed.at[b], spread.at[me], sp_send.at[b * rows_of + far], sp_recv.at[me],
            (z, b, far * pair + core),
        )

    def forward_copy(source):
        return remote(
            spread.at[source], spread.at[source], fw_send.at[source], sp_recv.at[source], sibling
        )

    inverse_copy.wait_recv()
    inv_scale = inverse_in[:, 0:1]
    for step in order:
        row_copy(step).wait_recv()
        b = mate(step)[0]
        at = pl.ds(pl.multiple_of(b * depth, 128), depth)
        normed[b] = (raw_rows[b].astype(F32) * inv_scale * gain[:, at]).astype(BF16)
        if step == 0:
            spread[me] = normed[g]
            if pair == 2:
                forward_copy(me).start()

        @pl.loop(1 if step == 0 else 0, rows_of)
        def _(turn):
            spread_copy(step, turn).start()

    relay = remote(tokens, arrived, row_send.at[batches], row_recv.at[batches], after)
    relay.start()
    early[3].wait()
    logits = jnp.zeros((slots, 1), F32)
    for b in range(batches):
        logits = logits + jnp.sum(
            raw_rows[b].astype(F32) * router[:, b * depth : (b + 1) * depth].astype(F32),
            axis=1, keepdims=True,
        )
    gate = jax.nn.sigmoid(logits)

    def arrived_from(buffer, sems, index):
        remote(buffer.at[index], buffer.at[index], sems.at[index], sems.at[index], after).wait_recv()

    for step in range(1, batches):
        arrived_from(picks, pick_recv, mate(step)[0])
    flats = [flat_slots(picks[b, 0:1, :count], shards, slots, tok_dev) for b in range(batches)]
    flat_cols = [as_column(flat) for flat in flats]

    half = batches * rows_of

    def same_core(step):
        index = lax.rem(g * rows_of + row + step, half)
        return lax.div(index, rows_of), lax.rem(index, rows_of)

    @pl.loop(1, half)
    def _(step):
        b, far = same_core(step)
        source = b * shards + far * pair + core
        arrived_from(spread, sp_recv, source)
        if pair == 2:
            forward_copy(source).start()

    if pair == 2:

        @pl.loop(0, half)
        def _(step):
            b, far = same_core(step)
            arrived_from(spread, sp_recv, b * shards + far * pair + 1 - core)

    for b in range(batches):
        choose = ones_where(flat_cols[b] == iota_f32((count, shards * slots), 1))
        source = spread[b * shards : (b + 1) * shards].reshape(shards * slots, depth)
        compact[b * count : (b + 1) * count, :] = nn_dot(choose, source).astype(BF16)

    pieces, cols = part.shape[1], head_cols // part.shape[1]

    def joint_copy(step, piece):
        index, device = mate(step)
        return remote(
            part.at[index, piece], joint.at[g, piece],
            jt_send.at[step, piece], jt_recv.at[g, piece], device,
        )

    def attended_copy(step, piece):
        device = mate(step)[1]
        return remote(
            attended.at[piece], both.at[g, piece],
            at_send.at[step, piece], at_recv.at[g, piece], device,
        )

    def arrived_piece(buffer, sems, index, piece):
        slot, sem = buffer.at[index, piece], sems.at[index, piece]
        remote(slot, slot, sem, sem, after).wait_recv()

    for which in range(3):
        loads[which].wait()

    @pl.loop(0, pieces)
    def _(piece):
        for which in range(3):
            at = pl.ds(pl.multiple_of(piece * cols, cols), cols)
            product = nn_dot(compact[...], w_in[which, :, at]).astype(BF16)
            for b in range(batches):
                part[b, piece, :, which * cols : (which + 1) * cols] = product[
                    b * count : (b + 1) * count
                ]
        for step in range(1, batches):
            joint_copy(step, piece).start()

    def rope(value):
        swapped = jnp.concatenate([value[:, HD // 2 :], value[:, : HD // 2]], axis=1)
        return (value * cosine + swapped * sine).astype(BF16)

    causal = lax.broadcasted_iota(jnp.int32, (count, count), 1) <= lax.broadcasted_iota(
        jnp.int32, (count, count), 0
    )
    for piece in range(pieces):
        total = part[g, piece].astype(F32)
        for step in range(1, batches):
            index = mate(step)[0]
            arrived_piece(joint, jt_recv, index, piece)
            total = total + joint[index, piece].astype(F32)
        for head in range(cols // HD):
            query, key, value = (
                total[:, which * cols + head * HD : which * cols + (head + 1) * HD]
                for which in range(3)
            )
            scores = nt_dot(rope(query), rope(key)) * HD ** (-0.5)
            scores = jnp.where(causal, scores, NEG_FILL)
            exponent = jnp.exp(scores - jnp.max(scores, axis=1, keepdims=True))
            weights = (exponent / jnp.sum(exponent, axis=1, keepdims=True)).astype(BF16)
            attended[piece, :, head * HD : (head + 1) * HD] = nn_dot(
                weights, value.astype(BF16)
            ).astype(BF16)
        for step in range(1, batches):
            attended_copy(step, piece).start()
        both[g, piece] = attended[piece]

    loads[3].wait()

    def middle_copy(batch, far):
        index = batch * shards + far * pair + 1 - core
        slot = batch * rows_of + far
        return remote(
            out_part.at[index], middle.at[slot], md_send.at[slot], md_recv.at[slot], sibling
        )

    def return_copy(batch, far):
        place = far * pair + core
        return remote(
            out_part.at[batch * shards + place], returned.at[g * rows_of + row],
            rt_send.at[batch * rows_of + far], rt_recv.at[g * rows_of + row], (z, batch, place),
        )

    def send_sums(step):
        batch = mate(step)[0]

        @pl.loop(0, rows_of)
        def _(turn):
            far = lax.rem(row + 1 + turn, rows_of)
            index = batch * shards + far * pair + core
            if pair == 2:
                arrived_from(middle, md_recv, batch * rows_of + far)
                out_part[index] = (
                    out_part[index].astype(F32) + middle[batch * rows_of + far].astype(F32)
                ).astype(BF16)
            if step:
                return_copy(batch, far).start()
            else:

                @pl.when(turn < rows_of - 1)
                def _():
                    return_copy(batch, far).start()

    out_cols = min(256, depth)
    for step in range(batches):
        batch = mate(step)[0]
        place = flat_slots(picks[batch, 0:1, :count], shards, slots, tok_dev)
        place = ones_where(place == iota_f32((shards * slots, count), 0))
        for piece in range(pieces):
            if step:
                arrived_piece(both, at_recv, batch, piece)
            slot_att[:, piece * cols : (piece + 1) * cols] = nn_dot(
                place, both[batch, piece]
            ).astype(BF16)

        @pl.loop(0, depth // out_cols)
        def _(block):
            start = pl.multiple_of(block * out_cols, out_cols)
            at = pl.ds(start, out_cols)
            product = nt_dot(slot_att[...], w_back[at, :]).astype(BF16)
            for owner in range(shards):
                out_part[batch * shards + owner, :, at] = product[
                    owner * slots : (owner + 1) * slots
                ]

        if pair == 2:

            @pl.loop(0, rows_of)
            def _(turn):
                middle_copy(batch, lax.rem(row + 1 + turn, rows_of)).start()

        if step:
            send_sums(step - 1)
    send_sums(batches - 1)
    returned[g * rows_of + row] = out_part[me]
    by_slot, by_row = local_onehots(my_picks, lowest, slots, tok_dev)
    scatter = nt_dot(by_row, by_slot).astype(BF16)
    held = jnp.sum(by_row.astype(F32), axis=1, keepdims=True) > 0.5
    relay.wait_recv()

    for step in range(batches):
        b = mate(step)[0]

        @pl.loop(1 if step == 0 else 0, rows_of)
        def _(turn):
            arrived_from(returned, rt_recv, b * rows_of + lax.rem(row + turn, rows_of))

        at = pl.ds(pl.multiple_of(b * depth, 128), depth)
        delta = returned[b * rows_of].astype(F32)
        for far in range(1, rows_of):
            delta = delta + returned[b * rows_of + far].astype(F32)
        delta = delta.astype(BF16).astype(F32)
        updated = (raw_rows[b].astype(F32) + gate * delta).astype(BF16)
        replaced = nn_dot(scatter, updated)
        out[:, at] = jnp.where(held, replaced, arrived[:, at].astype(F32)).astype(BF16)

    pick_back.wait_send()
    inverse_copy.wait_send()
    relay.wait_send()
    for step in range(batches):
        row_copy(step).wait_send()

        @pl.loop(1 if step == 0 else 0, rows_of)
        def _(turn):
            spread_copy(step, turn).wait_send()
            return_copy(mate(step)[0], lax.rem(row + turn, rows_of)).wait_send()

    for step in range(1, batches):
        pick_copy(step).wait_send()
        for piece in range(pieces):
            attended_copy(step, piece).wait_send()
            joint_copy(step, piece).wait_send()

    if pair == 2:

        @pl.loop(0, half)
        def _(step):
            b, far = same_core(step)
            forward_copy(b * shards + far * pair + core).wait_send()
            middle_copy(b, far).wait_send()


def per_device(incoming, chosen, norm_gain, router, w_query, w_key, w_value, w_out_t):
    sections = lax.axis_size("section")
    batches = lax.axis_size("dp")
    shards = lax.axis_size("seq")
    plane = batches * shards
    tok_dev, width = incoming.shape[2:]
    count = chosen.shape[2]
    slots = tok_dev // 4
    depth, head_cols = w_query.shape[1:]
    pair = 2 if shards % 2 == 0 else 1
    half = batches * (shards // pair)
    pieces = max(1, head_cols // 256)
    cols = head_cols // pieces
    pick_cols = -(-count // 128) * 128
    vmem = pl.BlockSpec(memory_space=pltpu.VMEM)
    hbm = pl.BlockSpec(memory_space=pl.ANY)
    dma = pltpu.SemaphoreType.DMA
    result = pl.pallas_call(
        functools.partial(kernel, sections, batches, shards),
        out_shape=jax.ShapeDtypeStruct((tok_dev, width), BF16),
        in_specs=[hbm] * 8,
        out_specs=vmem,
        scratch_shapes=[
            pltpu.VMEM((tok_dev, width), BF16),
            pltpu.VMEM((1, count), jnp.int32),
            pltpu.VMEM((1, width), F32),
            pltpu.VMEM((1, width), BF16),
            pltpu.VMEM((3, depth, head_cols), BF16),
            pltpu.VMEM((depth, head_cols), BF16),
            pltpu.VMEM((slots, 128), F32),
            pltpu.VMEM((slots, 128), F32),
            pltpu.VMEM((batches, 8, pick_cols), jnp.int32),
            pltpu.VMEM((8, pick_cols), jnp.int32),
            pltpu.VMEM((batches, slots, depth), BF16),
            pltpu.VMEM((batches, slots, depth), BF16),
            pltpu.VMEM((tok_dev, width), BF16),
            pltpu.VMEM((batches, slots, depth), BF16),
            pltpu.VMEM((plane, slots, depth), BF16),
            pltpu.VMEM((batches * count, depth), BF16),
            pltpu.VMEM((batches, pieces, count, 3 * cols), BF16),
            pltpu.VMEM((batches, pieces, count, 3 * cols), BF16),
            pltpu.VMEM((pieces, count, cols), BF16),
            pltpu.VMEM((batches, pieces, count, cols), BF16),
            pltpu.VMEM((shards * slots, head_cols), BF16),
            pltpu.VMEM((plane, slots, depth), BF16),
            pltpu.VMEM((half, slots, depth), BF16),
            pltpu.VMEM((half, slots, depth), BF16),
            dma((8,)),
            dma((batches,)), dma((batches + 1,)),
            dma((batches + 2,)), dma((batches + 2,)),
            dma((half,)), dma((plane,)), dma((plane,)),
            dma((batches, pieces)), dma((batches, pieces)),
            dma((batches, pieces)), dma((batches, pieces)),
            dma((half,)), dma((half,)), dma((half,)), dma((half,)),
        ],
        compiler_params=pltpu.CompilerParams(
            collective_id=0, has_side_effects=True, vmem_limit_bytes=64 * 1024 * 1024
        ),
    )(
        incoming[0, 0], chosen[0], norm_gain, router,
        w_query[0], w_key[0], w_value[0], w_out_t[0],
    )
    return result[None, None]


def solution(mesh):
    in_specs = (
        P("section", "dp", "seq", None),
        P("section", "dp", None),
        P("section", None),
        P("section", None),
        P("section", "dp", "seq"),
        P("section", "dp", "seq"),
        P("section", "dp", "seq"),
        P("section", "dp", "seq"),
    )
    out_specs = P("section", "dp", "seq", None)
    return jax.shard_map(
        per_device, mesh=mesh, in_specs=in_specs, out_specs=out_specs, check_vma=False
    )
```
